32 devices in a mesh: lon: 4 (over z), lat: 4 (over x, core), mp: 2 (over y).
Axes of the slice: x: 2, y: 2, z: 4, core: 2. Of those that a mesh axis runs over, the one named last changes fastest.
Arguments:
- fields: bfloat16 [160, 32, 2240], P('lat', 'lon', 'mp'), may hold values from -6 to 6
- shift_offsets: int32 [20], replicated, may hold values from 1 to 7, as said below
- w_embed: bfloat16 [2240, 1536], P('mp'), may hold values from -0.125 to 0.125
- w_qkv: bfloat16 [1536, 3, 768], P(None, None, 'mp'), may hold values from -0.15625 to 0.15625
- w_proj: bfloat16 [768, 1536], P('mp'), may hold values from -0.21875 to 0.21875
- w_head: bfloat16 [1536, 1120], P('mp'), may hold values from -0.15625 to 0.15625
- log_scale: float32 [12], P('mp'), may hold values from 1.6 to 5.3
- bias_table: float32 [12, 225], P('mp'), may hold values from -130 to 130
- cotangent: bfloat16 [160, 32, 1120], P(('lat', 'mp'), 'lon'), may hold values from -0.3125 to 0.3125
Outputs:
- prediction: bfloat16 [160, 32, 1120], P(('lat', 'mp'), 'lon')
- grad_qkv: float32 [1536, 3, 768], P(('lon', 'lat'), None, 'mp')
- grad_proj: float32 [768, 1536], P('mp', ('lon', 'lat'))
The draws below stay inside these ranges and needn't reach their ends.
Inputs may be any that keep to these rules, and one draw needn't show every extreme that they name: `shift_offsets`: in every draw some row of windows has the shift 7.
All inputs are finite; a program needn't handle non-finite values.
Results may differ from the reference program's by a relative error of at most 0.035.
Values may be sent and summed in bfloat16 or wider, within the bound.
No kernel may reach another device: no remote copies, remote signals or barrier semaphores. Data moves between devices by JAX's collectives and lax.ppermute only.
A program may use at most 128 MiB of HBM per device.

```python
import jax
import jax.numpy as jnp
from jax import lax

C = 1536
HEADS = 12
HD = 64
WIN = 8
EMB_IN = 2240
HEAD_OUT = 1120
ATT = 768
NLAT = 160
NLON = 32
ROWS_WIN = 20
ENTRIES = 225


def draw_shift_offsets(key, part):
    key = jax.random.fold_in(key, 11)
    first, second = jax.random.split(key)
    values = jax.random.randint(first, (ROWS_WIN,), 1, WIN)
    place = jax.random.randint(second, (), 0, ROWS_WIN)
    return jnp.where(jnp.arange(ROWS_WIN) == place, WIN - 1, values).astype(jnp.int32)


def draw_bias_table(key, part):
    key = jax.random.fold_in(key, 23)
    keys = jax.random.split(key, 1)
    base = 2.0 * jax.random.normal(keys[0], (HEADS, ENTRIES), jnp.float32)
    return base


def block_scale(rng, dims, cuts, least, top_value):
    def one(axis_at, parts):
        heights = jax.random.uniform(jax.random.fold_in(jax.random.fold_in(rng, 6), axis_at), (parts,), jnp.float32, least / len(cuts), top_value / len(cuts))
        return jnp.repeat(jnp.exp(heights), dims[axis_at] // parts).reshape((-1,) + (1,) * (len(dims) - axis_at - 1))

    loudness = one(*cuts[0])
    for cut in cuts[1:]:
        loudness = loudness * one(*cut)
    return loudness


def centred(own_key, dims, width, most, shards=(), kind=jnp.bfloat16):
    loudness = block_scale(own_key, dims, shards, -0.22, 0.18) if shards else 1.0
    values = jax.random.normal(own_key, dims, jnp.float32) * width * loudness
    return jnp.minimum(jnp.maximum(values, -most), most).astype(kind)


def setup_inputs(seed: int = 0) -> dict:
    key_of = jax.random.split(jax.random.key(seed), 10)
    return {
        "fields": centred(key_of[0], (NLAT, NLON, EMB_IN), 1.0, 6.0, ((0, 4), (1, 4), (2, 2))),
        "shift_offsets": draw_shift_offsets(jax.random.fold_in(key_of[9], 71), 0),
        "w_embed": centred(key_of[2], (EMB_IN, C), EMB_IN ** -0.5, 0.125, ((0, 2),)),
        "w_qkv": centred(key_of[3], (C, 3, ATT), C ** -0.5, 0.15625, ((2, 2),)),
        "w_proj": centred(key_of[4], (ATT, C), ATT ** -0.5, 0.21875, ((0, 2),)),
        "w_head": centred(key_of[5], (C, HEAD_OUT), C ** -0.5, 0.15625, ((0, 2),)),
        "log_scale": jnp.clip(1.6 + 3.7000002 * jax.random.uniform(key_of[6], (HEADS,), jnp.float32) ** block_scale(key_of[6], (HEADS,), ((0, 2),), -0.2, 0.2), 1.6, 5.3),
        "bias_table": draw_bias_table(jax.random.fold_in(key_of[9], 71), 0),
        "cotangent": centred(key_of[8], (NLAT, NLON, HEAD_OUT), (4.0 / (NLAT * NLON) ** 0.5), 0.3125, ((0, 8), (1, 4))),
    }


eps = 1e-06
scale_cap = 4.605170185988092

def offset_onehot(window):
    span = window * window
    places = jnp.arange(span, dtype=jnp.int32)
    across = places // window
    along = places % window
    code = (across[:, None] - across[None, :] + window - 1) * (2 * window - 1) + (along[:, None] - along[None, :] + window - 1)
    entries = jnp.arange((2 * window - 1) ** 2, dtype=jnp.int32)
    return (code[:, :, None] == entries[None, None, :]).astype(jnp.float32)

def window_attention(query_rows, key_rows, value_rows, scales, biases):
    query_f = query_rows.astype(jnp.float32)
    key_f = key_rows.astype(jnp.float32)
    value_f = value_rows.astype(jnp.float32)
    query_n = query_f * lax.rsqrt(lax.optimization_barrier(jnp.sum(query_f * query_f, -1, keepdims=True)) + eps)
    key_n = key_f * lax.rsqrt(lax.optimization_barrier(jnp.sum(key_f * key_f, -1, keepdims=True)) + eps)
    scores = jnp.einsum('wihd,wjhd->whij', query_n, key_n) * scales[None, :, None, None] + biases[None]
    top = lax.optimization_barrier(jnp.max(scores, -1, keepdims=True))
    weights = jnp.exp(scores - top)
    probs = (weights / lax.optimization_barrier(jnp.sum(weights, -1, keepdims=True))).astype(jnp.bfloat16)
    return jnp.einsum('whij,wjhd->wihd', probs.astype(jnp.float32), value_f)

def to_windows(grid, window):
    height, breadth, channels = grid.shape
    blocks = grid.reshape(height // window, window, breadth // window, window, channels)
    return blocks.transpose(0, 2, 1, 3, 4).reshape(-1, window * window, channels)

def from_windows(blocks, height, breadth, window):
    channels = blocks.shape[2]
    grid = blocks.reshape(height // window, breadth // window, window, window, channels)
    return grid.transpose(0, 2, 1, 3, 4).reshape(height, breadth, channels)

def roll_rows(grid, offsets, sign):
    groups = offsets.shape[0]
    blocks = grid.reshape(groups, grid.shape[0] // groups, grid.shape[1], grid.shape[2])
    moved = jax.vmap(lambda block, amount: jnp.roll(block, sign * amount, axis=1))(blocks, offsets)
    return moved.reshape(grid.shape)

def reference(fields, shift_offsets, w_embed, w_qkv, w_proj, w_head, log_scale, bias_table, cotangent):
    height, breadth = (fields.shape[0], fields.shape[1])
    total = height * breadth
    span = WIN * WIN
    embedded = jnp.dot(fields.reshape(total, EMB_IN), w_embed, preferred_element_type=jnp.float32)
    embedded = embedded.astype(jnp.bfloat16).reshape(height, breadth, C)
    rolled = roll_rows(embedded, shift_offsets, -1)
    win_tokens = to_windows(rolled, WIN).reshape(total, C)
    count_win = total // span
    qkv = jnp.dot(win_tokens, w_qkv.reshape(C, 3 * ATT), preferred_element_type=jnp.float32)
    qkv = qkv.astype(jnp.bfloat16).reshape(count_win, span, 3, HEADS, HD)
    scales = jnp.exp(jnp.minimum(log_scale, scale_cap))
    biases = jnp.einsum('ije,he->hij', offset_onehot(WIN), bias_table, precision=lax.Precision.HIGHEST)

    def attend(query_rows, key_rows, value_rows):
        return window_attention(query_rows, key_rows, value_rows, scales, biases)
    out_f, pullback = jax.vjp(attend, qkv[:, :, 0], qkv[:, :, 1], qkv[:, :, 2])
    attended = out_f.astype(jnp.bfloat16).reshape(total, ATT)
    mixed = jnp.dot(attended, w_proj, preferred_element_type=jnp.float32).astype(jnp.bfloat16)
    mixed_grid = from_windows(mixed.reshape(count_win, span, C), height, breadth, WIN)
    restored = roll_rows(mixed_grid, shift_offsets, 1)
    merged = (embedded.astype(jnp.float32) + restored.astype(jnp.float32)).astype(jnp.bfloat16)
    prediction = jnp.dot(merged.reshape(total, C), w_head, preferred_element_type=jnp.float32)
    prediction = prediction.astype(jnp.bfloat16).reshape(height, breadth, HEAD_OUT)
    upstream = lax.dot_general(cotangent.reshape(total, HEAD_OUT), w_head, (((1,), (1,)), ((), ())), preferred_element_type=jnp.float32)
    upstream = upstream.astype(jnp.bfloat16).reshape(height, breadth, C)
    upstream_rolled = to_windows(roll_rows(upstream, shift_offsets, -1), WIN).reshape(total, C)
    grad_proj = lax.dot_general(attended, upstream_rolled, (((0,), (0,)), ((), ())), preferred_element_type=jnp.float32)
    d_attended = lax.dot_general(upstream_rolled, w_proj, (((1,), (1,)), ((), ())), preferred_element_type=jnp.float32)
    d_attended = d_attended.astype(jnp.bfloat16).reshape(count_win, span, HEADS, HD)
    d_query, d_key, d_value = pullback(d_attended.astype(jnp.float32))
    d_qkv = jnp.stack([d_query, d_key, d_value], 2).reshape(total, 3 * ATT)
    grad_qkv = lax.dot_general(win_tokens, d_qkv, (((0,), (0,)), ((), ())), preferred_element_type=jnp.float32)
    return (prediction, grad_qkv.reshape(C, 3, ATT), grad_proj)
```

```python
import functools

import jax
import jax.numpy as jnp
from jax import lax
from jax.experimental import pallas as pl
from jax.experimental.pallas import tpu as pltpu
from jax.sharding import PartitionSpec as P

HD = 64
WIN = 8
SPAN = WIN * WIN
PAIR = 2 * HD

eps = 1e-06
scale_cap = 4.605170185988092

BF = jnp.bfloat16
F32 = jnp.float32
F16 = jnp.float16
TERM_SCALE = 64.0
VMEM_LIMIT = 30 * 1024 * 1024
SMALL_LIMIT = 24 * 1024 * 1024


def moved(value, axis, steps):
    count = lax.axis_size(axis)
    pairs = [(source, (source + steps) % count) for source in range(count)]
    return lax.ppermute(value, axis, pairs)


def swapped(value, axis, bit):
    count = lax.axis_size(axis)
    return lax.ppermute(value, axis, [(source, source ^ bit) for source in range(count)])


def spec(space=pltpu.VMEM):
    return pl.BlockSpec(memory_space=space)


def call(body, out_shape, kinds, micros, scratch=(), limit=VMEM_LIMIT):
    return pl.pallas_call(
        body,
        out_shape=out_shape,
        in_specs=[spec(pltpu.SMEM) if kind == "s" else spec() for kind in kinds],
        out_specs=jax.tree.map(lambda _: spec(), out_shape),
        scratch_shapes=list(scratch),
        compiler_params=pltpu.CompilerParams(vmem_limit_bytes=limit),
        cost_estimate=pl.CostEstimate(flops=int(micros * 1.0e9), bytes_accessed=1, transcendentals=0),
    )


def after(value, *others):
    return lax.optimization_barrier((value,) + others)[0]


def shape(dims, dtype=BF):
    return jax.ShapeDtypeStruct(tuple(dims), dtype)


def dot(a, b, ca=1, cb=0):
    return lax.dot_general(a, b, (((ca,), (cb,)), ((), ())), preferred_element_type=F32)


def rolled_block(own, other, shift):
    size = own.shape[0]
    row = lax.broadcasted_iota(jnp.int32, (size, size), 0)
    col = lax.broadcasted_iota(jnp.int32, (size, size), 1)
    target = (row & (WIN - 1)) + shift
    same = ((row >> 3) == (col >> 3)) & ((col & (WIN - 1)) == (target & (WIN - 1)))
    inside = (target >= 0) & (target < WIN)
    mine = jnp.where(same & inside, 1.0, 0.0).astype(BF)
    theirs = jnp.where(same & ~inside, 1.0, 0.0).astype(BF)
    return (dot(mine, own) + dot(theirs, other)).astype(BF)


def roll_kernel(sign, shifts, own, other, out):
    for block in range(own.shape[0]):
        out[block] = rolled_block(own[block], other[block], sign * shifts[block])


def roll_call(shifts, own, other, sign):
    body = functools.partial(roll_kernel, sign)
    return call(body, jax.ShapeDtypeStruct(own.shape, BF), "svv", 2)(shifts, own, other)


def embed_kernel(shifts, own, other, weight, out, gathered):
    for block in range(own.shape[0]):
        gathered[pl.ds(block * SPAN, SPAN), :] = rolled_block(
            own[block], other[block], shifts[block]
        )
    out[...] = dot(gathered[...], weight[...]) * TERM_SCALE


def embed_call(shifts, own, other, weight):
    rows = own.shape[0] * SPAN
    width = weight.shape[1]
    return call(
        embed_kernel,
        jax.ShapeDtypeStruct((rows, width), F32),
        "svvv",
        5,
        [pltpu.VMEM((rows, weight.shape[0]), BF)],
    )(shifts, own, other, weight)


def halves(value):
    left = lax.broadcasted_iota(jnp.int32, value.shape, 1) < HD
    zero = jnp.zeros_like(value)
    return jnp.concatenate([jnp.where(left, value, zero), jnp.where(left, zero, value)], 0)


def joined(value):
    top = value[:SPAN]
    left = lax.broadcasted_iota(jnp.int32, top.shape, 1) < HD
    return jnp.where(left, top, value[SPAN:])


def two_parts(value):
    high = value.astype(BF)
    return high, (value - high.astype(F32)).astype(BF)


def head_ones():
    row = lax.broadcasted_iota(jnp.int32, (PAIR, PAIR), 0)
    col = lax.broadcasted_iota(jnp.int32, (PAIR, PAIR), 1)
    return jnp.where((row < HD) == (col < HD), 1.0, 0.0).astype(BF)


def head_sums(value, ones):
    high, low = two_parts(value)
    return dot(high, ones) + dot(low, ones)


def square(value):
    wide = value.astype(F32)
    return wide * wide


def row_norms(query_halves):
    high, low = two_parts(square(query_halves))
    ones = jnp.ones((WIN, PAIR), BF)
    total = dot(ones, high, 1, 1) + dot(ones, low, 1, 1)
    return lax.rsqrt(total[:1] + eps)


def forward_kernel(rolled, w_qkv, scales, biases, qkv, probs, attended):
    width = w_qkv.shape[2]
    for part in range(3):
        qkv[:, part * width : (part + 1) * width] = dot(rolled[...], w_qkv[part]).astype(BF)
    ones = head_ones()
    pairs = width // PAIR
    for window in range(rolled.shape[0] // SPAN):
        rows = pl.ds(window * SPAN, SPAN)
        for pair in range(pairs):
            lanes = pl.ds(pair * PAIR, PAIR)
            query = qkv[rows, lanes]
            key = qkv[rows, pl.ds(width + pair * PAIR, PAIR)]
            value = qkv[rows, pl.ds(2 * width + pair * PAIR, PAIR)]
            query_halves = halves(query)
            key_norm = lax.rsqrt(head_sums(square(key), ones) + eps)
            query_norm = row_norms(query_halves) * scales[pair]
            scores = dot(key, query_halves, 1, 1) * key_norm * query_norm + biases[pair]
            weights = jnp.exp(scores - jnp.max(scores, 0, keepdims=True))
            share = weights * (1.0 / jnp.sum(weights, 0, keepdims=True))
            probs[window, pair] = share
            attended[rows, lanes] = joined(dot(share.astype(BF), value, 0, 0)).astype(BF)


def forward_call(mine, theirs, w_qkv, scales, biases):
    rolled = ((mine.astype(F32) + theirs.astype(F32)) * (1.0 / TERM_SCALE)).astype(BF)
    rows = rolled.shape[0]
    width = w_qkv.shape[2]
    pairs = width // PAIR
    out_shape = (
        shape((rows, 3 * width)),
        shape((rows // SPAN, pairs, SPAN, PAIR), F32),
        shape((rows, width)),
    )
    got = call(forward_kernel, out_shape, "vvvv", 9)(rolled, w_qkv, scales, biases)
    return (rolled,) + tuple(got)


def unit_grad(value, norm, grad, ones):
    wide = value.astype(F32)
    along = head_sums(wide * grad, ones)
    return norm * (grad - wide * (norm * norm) * along)


def backward_kernel(chunks, place, own_up, other_up, w_proj, scales, *refs):
    width, model = w_proj.shape
    d_qk, d_value, d_att = refs[2 * chunks :]
    half = model // 2
    mine = pl.ds(pl.multiple_of(place[0] * half, PAIR), half)
    theirs = pl.ds(pl.multiple_of((1 - place[0]) * half, PAIR), half)
    d_att[...] = (
        dot(own_up[...], w_proj[:, mine], 1, 1) + dot(other_up[...], w_proj[:, theirs], 1, 1)
    ).astype(BF)
    first = 0
    for qkv, probs in zip(refs[:chunks], refs[chunks : 2 * chunks]):
        backward_chunk(first, qkv, probs, scales, d_att, d_qk, d_value)
        first += probs.shape[0]


def backward_chunk(first, qkv, probs, scales, d_att, d_qk, d_value):
    width = d_att.shape[1]
    ones = head_ones()
    for window in range(probs.shape[0]):
        rows = pl.ds((first + window) * SPAN, SPAN)
        for pair in range(width // PAIR):
            spots = [pl.ds(part * width + pair * PAIR, PAIR) for part in range(3)]
            query, key, value = [qkv[pl.ds(window * SPAN, SPAN), spot] for spot in spots]
            query_halves = halves(query)
            key_norm = lax.rsqrt(head_sums(square(key), ones) + eps)
            query_norm = lax.rsqrt(head_sums(square(query), ones) + eps)
            query_lanes = row_norms(query_halves)
            share = probs[window, pair]
            grad_halves = halves(d_att[rows, pl.ds(pair * PAIR, PAIR)])
            d_value[rows, spots[0]] = dot(share.astype(BF), grad_halves).astype(BF)
            d_probs = dot(value, grad_halves, 1, 1).astype(BF).astype(F32)
            mean = jnp.sum(d_probs * share, 0, keepdims=True)
            d_cos = share * (d_probs - mean) * scales[pair]
            d_query = joined(dot((d_cos * key_norm).astype(BF), key, 0, 0))
            d_key = dot((d_cos * query_lanes).astype(BF), query_halves)
            d_qk[rows, spots[0]] = unit_grad(query, query_norm, d_query, ones).astype(BF)
            d_qk[rows, spots[1]] = unit_grad(key, key_norm, d_key, ones).astype(BF)


def backward_call(place, own_up, other_up, w_proj, scales, qkv, probs):
    rows = own_up.shape[0]
    width = w_proj.shape[0]
    return call(
        functools.partial(backward_kernel, len(qkv)),
        (shape((rows, 2 * width)), shape((rows, width))),
        "svvvv" + "vv" * len(qkv),
        9,
        [pltpu.VMEM((rows, width), BF)],
        SMALL_LIMIT,
    )(place, own_up, other_up, w_proj, scales, *qkv, *probs)


def half_up_kernel(place, own, other, w_head_t, out):
    rows = own.shape[0]
    out[pl.ds(pl.multiple_of(place[0] * rows, 32), rows), :] = dot(own[...], w_head_t[...]).astype(BF)
    out[pl.ds(pl.multiple_of((1 - place[0]) * rows, 32), rows), :] = dot(
        other[...], w_head_t[...]
    ).astype(BF)


def half_up_call(place, own, other, w_head_t):
    rows, depth = own.shape
    width = w_head_t.shape[1]
    return call(
        half_up_kernel, shape((2 * rows, width)), "svvv", 3
    )(place, own, other, w_head_t)


def mix_kernel(chunks, place, w_proj, *refs):
    att, keep, send = refs[:chunks], refs[chunks], refs[chunks + 1]
    half = w_proj.shape[1] // 2
    mine = pl.ds(pl.multiple_of(place[0] * half, PAIR), half)
    theirs = pl.ds(pl.multiple_of((1 - place[0]) * half, PAIR), half)
    start = 0
    for a in att:
        rows = pl.ds(start, a.shape[0])
        send[rows, :] = dot(a[...], w_proj[:, theirs]).astype(BF)
        keep[rows, :] = dot(a[...], w_proj[:, mine]).astype(BF)
        start += a.shape[0]


def mix_call(place, w_proj, attended):
    count = sum(a.shape[0] for a in attended)
    width, model = w_proj.shape
    out = shape((count, model // 2))
    return call(
        functools.partial(mix_kernel, len(attended)),
        (out, out),
        "sv" + "v" * len(attended),
        3,
    )(place, w_proj, *attended)


def head_kernel(chunks, place, mine, theirs, w_head_t, *refs):
    rolled, keep, send, merged = refs[:chunks], refs[chunks], refs[chunks + 1], refs[chunks + 2]
    half = w_head_t.shape[1]
    lanes = pl.ds(pl.multiple_of(place[0] * half, PAIR), half)
    start = 0
    for a in rolled:
        rows = pl.ds(start, a.shape[0])
        mixed = (mine[rows, :].astype(F32) + theirs[rows, :].astype(F32)).astype(BF)
        merged[rows, :] = (a[:, lanes].astype(F32) + mixed.astype(F32)).astype(BF)
        start += a.shape[0]
    count = keep.shape[0]
    own = pl.ds(pl.multiple_of(place[0] * count, 32), count)
    other = pl.ds(pl.multiple_of((1 - place[0]) * count, 32), count)
    send[...] = dot(merged[other, :], w_head_t[...], 1, 1).astype(BF)
    keep[...] = dot(merged[own, :], w_head_t[...], 1, 1).astype(BF)


def head_call(place, mine, theirs, w_head_t, rolled):
    count, half = mine.shape
    outputs = w_head_t.shape[0]
    out = shape((count // 2, outputs))
    return call(
        functools.partial(head_kernel, len(rolled)),
        (out, out),
        "svvv" + "v" * len(rolled),
        4,
        [pltpu.VMEM((count, half), BF)],
    )(place, mine, theirs, w_head_t, *rolled)


def offset_onehot(window):
    span = window * window
    places = jnp.arange(span, dtype=jnp.int32)
    across = places // window
    along = places % window
    code = (across[:, None] - across[None, :] + window - 1) * (2 * window - 1) + (
        along[:, None] - along[None, :] + window - 1
    )
    entries = jnp.arange((2 * window - 1) ** 2, dtype=jnp.int32)
    return (code[:, :, None] == entries[None, None, :]).astype(F32)


def bits_of(axis):
    bits = []
    bit = 1
    while bit < lax.axis_size(axis):
        bits.append((axis, bit))
        bit *= 2
    return bits


def my_bit(axis, bit):
    return (lax.axis_index(axis) // bit) % 2


class Sum:
    def __init__(self, keep, send, order):
        self.dims = [("lon", bit) for _, bit in reversed(bits_of("lon"))]
        self.dims += [("lat", bit) for _, bit in reversed(bits_of("lat"))][:-1]
        self.rows = keep.shape[1:]
        self.order = list(order)
        self.keep = keep
        self.got = swapped(send, "lat", 1)

    def step(self):
        axis, bit = self.order.pop(0)
        place = self.dims.index((axis, bit))
        cut = (2,) * len(self.dims) + self.rows
        keep, got = self.keep.reshape(cut), self.got.reshape(cut)
        mine = my_bit(axis, bit)

        def total(index):
            a = lax.dynamic_index_in_dim(keep, index, place, keepdims=False)
            b = lax.dynamic_index_in_dim(got, index, place, keepdims=False)
            return (a.astype(F32) + b.astype(F32)).astype(BF)

        send = total(1 - mine)
        self.keep = total(mine)
        self.got = swapped(send, axis, bit)
        self.dims.pop(place)
        return send

    def result(self):
        while self.order:
            self.step()
        return self.keep.reshape(self.rows).astype(F32) + self.got.reshape(self.rows).astype(F32)


def cut_pieces(value, pieces, axis):
    size = value.shape[axis] // pieces
    value = value.reshape(value.shape[:axis] + (pieces // 2, 2, size) + value.shape[axis + 1 :])
    low = my_bit("lat", 1)
    return [lax.dynamic_index_in_dim(value, bit, axis + 1, keepdims=False) for bit in (low, 1 - low)]


def local(fields, shift_offsets, w_embed, w_qkv, w_proj, w_head, log_scale, bias_table, cotangent):
    height, breadth, depth = fields.shape
    groups = height // WIN
    model = w_embed.shape[1]
    outputs = w_head.shape[1]
    width = w_qkv.shape[2]
    pairs = width // PAIR
    lat, mp = lax.axis_index("lat"), lax.axis_index("mp")
    rows_here = cotangent.shape[0]
    offsets = lax.dynamic_slice_in_dim(shift_offsets, lat * groups, groups)
    strip = 4
    strips = rows_here // strip
    firsts = mp * rows_here + strip * jnp.arange(strips, dtype=jnp.int32)
    strip_offsets = jnp.take(offsets, firsts // WIN)
    place = mp.reshape(1)
    pieces = lax.axis_size("lon") * lax.axis_size("lat")
    z_bits = bits_of("lon")
    x_bits = bits_of("lat")[1:]

    cuts = [0, 2, groups]
    tiles = fields.reshape(groups, SPAN, depth)
    tiles = [tiles[first:last] for first, last in zip(cuts[:-1], cuts[1:])]
    shifts = [offsets[first:last] for first, last in zip(cuts[:-1], cuts[1:])]
    cot = cotangent.reshape(-1, outputs)
    next_tiles = [moved(tile, "lon", -1) for tile in tiles]
    other_cot = swapped(cot, "mp", 1)

    scales = jnp.exp(jnp.minimum(log_scale, scale_cap))
    scales = jnp.repeat(scales.reshape(pairs, 1, 2), HD, axis=2)
    biases = jnp.einsum(
        "ije,he->hji", offset_onehot(WIN), bias_table, precision=lax.Precision.HIGHEST
    )
    biases = biases.reshape(pairs, 2, SPAN, SPAN).transpose(0, 2, 1, 3).reshape(pairs, SPAN, PAIR)

    half_up = half_up_call(place, cot, other_cot, w_head.T)
    next_tiles[0], half_up, biases = lax.optimization_barrier((next_tiles[0], half_up, biases))
    terms, other_terms = [], []
    for index, (shift, tile, next_tile) in enumerate(zip(shifts, tiles, next_tiles)):
        if terms:
            next_tile = after(next_tile, terms[-1])
            half_up = after(half_up, next_tile)
        terms.append(embed_call(shift, tile, next_tile, w_embed).astype(F16))
        other_terms.append(swapped(terms[-1], "mp", 1))
    half_up = half_up.reshape(groups, SPAN, -1)
    own_up = roll_call(offsets, half_up, moved(half_up, "lon", -1), 1)
    own_up = own_up.reshape(groups * SPAN, -1)
    other_up = swapped(after(own_up, other_terms[-1]), "mp", 1)

    w_parts = w_qkv.transpose(1, 0, 2)
    rolled, qkv, probs, attended = zip(
        *[forward_call(a, b, w_parts, scales, biases) for a, b in zip(terms, other_terms)]
    )
    mixed_here, mixed_there = mix_call(place, w_proj, attended)
    left_keep, left_send = [
        side.reshape(groups * SPAN, -1)
        for side in cut_pieces(jnp.concatenate(rolled, 0), pieces, 1)
    ]
    all_attended = jnp.concatenate(attended, 0)
    other_up, mixed_here, left_keep, left_send, all_attended = lax.optimization_barrier(
        (other_up, mixed_here, left_keep, left_send, all_attended)
    )
    mixed_got = swapped(after(mixed_there, other_up), "mp", 1)
    up = jnp.where(
        mp == 0, jnp.concatenate([own_up, other_up], 1), jnp.concatenate([other_up, own_up], 1)
    )
    keep, send = cut_pieces(dot(up, all_attended, 0, 0).astype(BF), pieces, 0)
    sum_p = Sum(keep, send, x_bits + z_bits)

    d_qk, d_value = backward_call(
        place, own_up, after(other_up, send), w_proj, scales, qkv, probs
    )

    def products(left, right):
        return dot(left, right, 0, 0).astype(BF).reshape(pieces // 2, model // pieces, -1)

    sum_p.got = after(sum_p.got, d_qk)
    sent = sum_p.step()
    pred_here, pred_there = head_call(place, after(mixed_here, sent), mixed_got, w_head.T, rolled)
    v_send = products(left_send, after(d_value, pred_there))
    sum_p.got = after(sum_p.got, v_send)
    sent = sum_p.step()
    qk_send = products(left_send, after(d_qk, sent))
    v_keep = products(left_keep, after(d_value, qk_send))
    sum_v = Sum(v_keep, v_send, x_bits + z_bits)
    sum_v.got = after(sum_v.got, qk_send)
    sent = sum_v.step()
    qk_keep = products(left_keep, after(d_qk, sent))
    sum_qk = Sum(qk_keep, qk_send, x_bits + z_bits)
    sum_qk.got = after(sum_qk.got, sent)
    sent = sum_qk.step()
    sum_p.got = after(sum_p.got, sent)
    sent = sum_p.step()
    pred_got = after(swapped(pred_there, "mp", 1), sent)
    pred = (pred_here.astype(F32) + pred_got.astype(F32)).astype(BF)
    pred = pred.reshape(strips, strip * WIN, outputs)
    before = moved(pred, "lon", 1)
    sum_v.got = after(sum_v.got, pred)
    sent = sum_v.step()
    sum_p.got = after(sum_p.got, sent)
    grad_proj = sum_p.result().T
    sum_v.got = after(sum_v.got, grad_proj)
    sent = sum_v.step()
    sum_qk.got = after(sum_qk.got, sent)
    sent = sum_qk.step()
    before = after(before, sent)
    prediction = roll_call(strip_offsets, pred, before, -1).reshape(rows_here, breadth, outputs)
    grad_v = sum_v.result()
    sum_qk.got = after(sum_qk.got, grad_v)
    grad_qk = sum_qk.result()
    grad_qkv = jnp.concatenate([grad_qk, grad_v], 1).reshape(-1, 3, width)
    return (prediction, grad_qkv, grad_proj)


def solution(mesh):
    in_specs = (
        P("lat", "lon", "mp"),
        P(),
        P("mp", None),
        P(None, None, "mp"),
        P("mp", None),
        P("mp", None),
        P("mp"),
        P("mp", None),
        P(("lat", "mp"), "lon", None),
    )
    out_specs = (
        P(("lat", "mp"), "lon", None),
        P(("lon", "lat"), None, "mp"),
        P("mp", ("lon", "lat")),
    )
    return jax.shard_map(local, mesh=mesh, in_specs=in_specs, out_specs=out_specs, check_vma=False)
```

```python
import functools

import jax
import jax.numpy as jnp
from jax import lax
from jax.experimental import pallas as pl
from jax.experimental.pallas import tpu as pltpu
from jax.sharding import PartitionSpec as P

HD = 64
WIN = 8
SPAN = WIN * WIN
PAIR = 2 * HD

eps = 1e-06
scale_cap = 4.605170185988092

BF = jnp.bfloat16
F32 = jnp.float32
F16 = jnp.float16
TERM_SCALE = 64.0
VMEM_LIMIT = 30 * 1024 * 1024
SMALL_LIMIT = 24 * 1024 * 1024


def moved(value, axis, steps):
    count = lax.axis_size(axis)
    pairs = [(source, (source + steps) % count) for source in range(count)]
    return lax.ppermute(value, axis, pairs)


def swapped(value, axis, bit):
    count = lax.axis_size(axis)
    return lax.ppermute(value, axis, [(source, source ^ bit) for source in range(count)])


def spec(space=pltpu.VMEM):
    return pl.BlockSpec(memory_space=space)


def call(body, out_shape, kinds, micros, scratch=(), limit=VMEM_LIMIT):
    return pl.pallas_call(
        body,
        out_shape=out_shape,
        in_specs=[spec(pltpu.SMEM) if kind == "s" else spec() for kind in kinds],
        out_specs=jax.tree.map(lambda _: spec(), out_shape),
        scratch_shapes=list(scratch),
        compiler_params=pltpu.CompilerParams(vmem_limit_bytes=limit),
        cost_estimate=pl.CostEstimate(flops=int(micros * 1.0e9), bytes_accessed=1, transcendentals=0),
    )


def after(value, *others):
    return lax.optimization_barrier((value,) + others)[0]


def shape(dims, dtype=BF):
    return jax.ShapeDtypeStruct(tuple(dims), dtype)


def dot(a, b, ca=1, cb=0):
    return lax.dot_general(a, b, (((ca,), (cb,)), ((), ())), preferred_element_type=F32)


def rolled_block(own, other, shift):
    size = own.shape[0]
    row = lax.broadcasted_iota(jnp.int32, (size, size), 0)
    col = lax.broadcasted_iota(jnp.int32, (size, size), 1)
    target = (row & (WIN - 1)) + shift
    same = ((row >> 3) == (col >> 3)) & ((col & (WIN - 1)) == (target & (WIN - 1)))
    inside = (target >= 0) & (target < WIN)
    mine = jnp.where(same & inside, 1.0, 0.0).astype(BF)
    theirs = jnp.where(same & ~inside, 1.0, 0.0).astype(BF)
    return (dot(mine, own) + dot(theirs, other)).astype(BF)


def roll_kernel(sign, shifts, own, other, out):
    for block in range(own.shape[0]):
        out[block] = rolled_block(own[block], other[block], sign * shifts[block])


def roll_call(shifts, own, other, sign):
    body = functools.partial(roll_kernel, sign)
    return call(body, jax.ShapeDtypeStruct(own.shape, BF), "svv", 2)(shifts, own, other)


def embed_kernel(shifts, own, other, weight, out, gathered):
    for block in range(own.shape[0]):
        gathered[pl.ds(block * SPAN, SPAN), :] = rolled_block(
            own[block], other[block], shifts[block]
        )
    out[...] = dot(gathered[...], weight[...]) * TERM_SCALE


def embed_call(shifts, own, other, weight):
    rows = own.shape[0] * SPAN
    width = weight.shape[1]
    return call(
        embed_kernel,
        jax.ShapeDtypeStruct((rows, width), F32),
        "svvv",
        5,
        [pltpu.VMEM((rows, weight.shape[0]), BF)],
    )(shifts, own, other, weight)


def halves(value):
    left = lax.broadcasted_iota(jnp.int32, value.shape, 1) < HD
    zero = jnp.zeros_like(value)
    return jnp.concatenate([jnp.where(left, value, zero), jnp.where(left, zero, value)], 0)


def joined(value):
    top = value[:SPAN]
    left = lax.broadcasted_iota(jnp.int32, top.shape, 1) < HD
    return jnp.where(left, top, value[SPAN:])


def two_parts(value):
    high = value.astype(BF)
    return high, (value - high.astype(F32)).astype(BF)


def head_ones():
    row = lax.broadcasted_iota(jnp.int32, (PAIR, PAIR), 0)
    col = lax.broadcasted_iota(jnp.int32, (PAIR, PAIR), 1)
    return jnp.where((row < HD) == (col < HD), 1.0, 0.0).astype(BF)


def short_sums(value, ones):
    return dot(value.astype(BF), ones)


def head_sums(value, ones):
    high, low = two_parts(value)
    return dot(high, ones) + dot(low, ones)


def square(value):
    wide = value.astype(F32)
    return wide * wide


def row_norms(query_halves):
    high, low = two_parts(square(query_halves))
    ones = jnp.ones((WIN, PAIR), BF)
    total = dot(ones, high, 1, 1) + dot(ones, low, 1, 1)
    return lax.rsqrt(total[:1] + eps)


def short_row_norms(query_halves):
    ones = jnp.ones((WIN, PAIR), BF)
    total = dot(ones, square(query_halves).astype(BF), 1, 1)
    return lax.rsqrt(total[:1] + eps)


def forward_kernel(rolled, w_qkv, scales, biases, qkv, probs, attended):
    width = w_qkv.shape[2]
    for part in range(3):
        qkv[:, part * width : (part + 1) * width] = dot(rolled[...], w_qkv[part]).astype(BF)
    ones = head_ones()
    pairs = width // PAIR
    for window in range(rolled.shape[0] // SPAN):
        rows = pl.ds(window * SPAN, SPAN)
        for pair in range(pairs):
            lanes = pl.ds(pair * PAIR, PAIR)
            query = qkv[rows, lanes]
            key = qkv[rows, pl.ds(width + pair * PAIR, PAIR)]
            value = qkv[rows, pl.ds(2 * width + pair * PAIR, PAIR)]
            query_halves = halves(query)
            key_norm = lax.rsqrt(head_sums(square(key), ones) + eps)
            query_norm = row_norms(query_halves) * scales[pair]
            scores = dot(key, query_halves, 1, 1) * key_norm * query_norm + biases[pair]
            weights = jnp.exp(scores - jnp.max(scores, 0, keepdims=True))
            share = weights * (1.0 / jnp.sum(weights, 0, keepdims=True))
            probs[window, pair] = share
            attended[rows, lanes] = joined(dot(share.astype(BF), value, 0, 0)).astype(BF)


def forward_call(mine, theirs, w_qkv, scales, biases):
    rolled = ((mine.astype(F32) + theirs.astype(F32)) * (1.0 / TERM_SCALE)).astype(BF)
    rows = rolled.shape[0]
    width = w_qkv.shape[2]
    pairs = width // PAIR
    out_shape = (
        shape((rows, 3 * width)),
        shape((rows // SPAN, pairs, SPAN, PAIR), F32),
        shape((rows, width)),
    )
    got = call(forward_kernel, out_shape, "vvvv", 0.05)(rolled, w_qkv, scales, biases)
    return (rolled,) + tuple(got)


def unit_grad(value, norm, grad, ones):
    wide = value.astype(F32)
    along = short_sums(wide * grad, ones)
    return norm * (grad - wide * (norm * norm) * along)


def backward_kernel(chunks, place, own_up, other_up, w_proj, scales, *refs):
    width, model = w_proj.shape
    d_qk, d_value, d_att = refs[2 * chunks :]
    half = model // 2
    mine = pl.ds(pl.multiple_of(place[0] * half, PAIR), half)
    theirs = pl.ds(pl.multiple_of((1 - place[0]) * half, PAIR), half)
    d_att[...] = (
        dot(own_up[...], w_proj[:, mine], 1, 1) + dot(other_up[...], w_proj[:, theirs], 1, 1)
    ).astype(BF)
    first = 0
    for qkv, probs in zip(refs[:chunks], refs[chunks : 2 * chunks]):
        backward_chunk(first, qkv, probs, scales, d_att, d_qk, d_value)
        first += probs.shape[0]


def backward_chunk(first, qkv, probs, scales, d_att, d_qk, d_value):
    width = d_att.shape[1]
    ones = head_ones()
    for window in range(probs.shape[0]):
        rows = pl.ds((first + window) * SPAN, SPAN)
        for pair in range(width // PAIR):
            spots = [pl.ds(part * width + pair * PAIR, PAIR) for part in range(3)]
            query, key, value = [qkv[pl.ds(window * SPAN, SPAN), spot] for spot in spots]
            query_halves = halves(query)
            key_norm = lax.rsqrt(short_sums(square(key), ones) + eps)
            query_norm = lax.rsqrt(short_sums(square(query), ones) + eps)
            query_lanes = short_row_norms(query_halves)
            share = probs[window, pair]
            grad_halves = halves(d_att[rows, pl.ds(pair * PAIR, PAIR)])
            d_value[rows, spots[0]] = dot(share.astype(BF), grad_halves).astype(BF)
            d_probs = dot(value, grad_halves, 1, 1).astype(BF).astype(F32)
            mean = jnp.sum(d_probs * share, 0, keepdims=True)
            d_cos = share * (d_probs - mean) * scales[pair]
            d_query = joined(dot((d_cos * key_norm).astype(BF), key, 0, 0))
            d_key = dot((d_cos * query_lanes).astype(BF), query_halves)
            d_qk[rows, spots[0]] = unit_grad(query, query_norm, d_query, ones).astype(BF)
            d_qk[rows, spots[1]] = unit_grad(key, key_norm, d_key, ones).astype(BF)


def backward_call(place, own_up, other_up, w_proj, scales, qkv, probs):
    rows = own_up.shape[0]
    width = w_proj.shape[0]
    return call(
        functools.partial(backward_kernel, len(qkv)),
        (shape((rows, 2 * width)), shape((rows, width))),
        "svvvv" + "vv" * len(qkv),
        9,
        [pltpu.VMEM((rows, width), BF)],
        SMALL_LIMIT,
    )(place, own_up, other_up, w_proj, scales, *qkv, *probs)


def half_up_kernel(place, own, other, w_head_t, out):
    rows = own.shape[0]
    out[pl.ds(pl.multiple_of(place[0] * rows, 32), rows), :] = dot(own[...], w_head_t[...]).astype(BF)
    out[pl.ds(pl.multiple_of((1 - place[0]) * rows, 32), rows), :] = dot(
        other[...], w_head_t[...]
    ).astype(BF)


def half_up_call(place, own, other, w_head_t):
    rows, depth = own.shape
    width = w_head_t.shape[1]
    return call(
        half_up_kernel, shape((2 * rows, width)), "svvv", 3
    )(place, own, other, w_head_t)


def mix_kernel(chunks, place, w_proj, *refs):
    att, keep, send = refs[:chunks], refs[chunks], refs[chunks + 1]
    half = w_proj.shape[1] // 2
    mine = pl.ds(pl.multiple_of(place[0] * half, PAIR), half)
    theirs = pl.ds(pl.multiple_of((1 - place[0]) * half, PAIR), half)
    start = 0
    for a in att:
        rows = pl.ds(start, a.shape[0])
        send[rows, :] = dot(a[...], w_proj[:, theirs]).astype(BF)
        keep[rows, :] = dot(a[...], w_proj[:, mine]).astype(BF)
        start += a.shape[0]


def mix_call(place, w_proj, attended):
    count = sum(a.shape[0] for a in attended)
    width, model = w_proj.shape
    out = shape((count, model // 2))
    return call(
        functools.partial(mix_kernel, len(attended)),
        (out, out),
        "sv" + "v" * len(attended),
        0.05,
    )(place, w_proj, *attended)


def head_kernel(chunks, place, mine, theirs, w_head_t, *refs):
    rolled, keep, send, merged = refs[:chunks], refs[chunks], refs[chunks + 1], refs[chunks + 2]
    half = w_head_t.shape[1]
    lanes = pl.ds(pl.multiple_of(place[0] * half, PAIR), half)
    start = 0
    for a in rolled:
        rows = pl.ds(start, a.shape[0])
        mixed = (mine[rows, :].astype(F32) + theirs[rows, :].astype(F32)).astype(BF)
        merged[rows, :] = (a[:, lanes].astype(F32) + mixed.astype(F32)).astype(BF)
        start += a.shape[0]
    count = keep.shape[0]
    own = pl.ds(pl.multiple_of(place[0] * count, 32), count)
    other = pl.ds(pl.multiple_of((1 - place[0]) * count, 32), count)
    send[...] = dot(merged[other, :], w_head_t[...], 1, 1).astype(BF)
    keep[...] = dot(merged[own, :], w_head_t[...], 1, 1).astype(BF)


def head_call(place, mine, theirs, w_head_t, rolled):
    count, half = mine.shape
    outputs = w_head_t.shape[0]
    out = shape((count // 2, outputs))
    return call(
        functools.partial(head_kernel, len(rolled)),
        (out, out),
        "svvv" + "v" * len(rolled),
        4,
        [pltpu.VMEM((count, half), BF)],
    )(place, mine, theirs, w_head_t, *rolled)


def offset_onehot(window):
    span = window * window
    places = jnp.arange(span, dtype=jnp.int32)
    across = places // window
    along = places % window
    code = (across[:, None] - across[None, :] + window - 1) * (2 * window - 1) + (
        along[:, None] - along[None, :] + window - 1
    )
    entries = jnp.arange((2 * window - 1) ** 2, dtype=jnp.int32)
    return (code[:, :, None] == entries[None, None, :]).astype(F32)


def bits_of(axis):
    bits = []
    bit = 1
    while bit < lax.axis_size(axis):
        bits.append((axis, bit))
        bit *= 2
    return bits


def my_bit(axis, bit):
    return (lax.axis_index(axis) // bit) % 2


class Sum:
    def __init__(self, keep, send, order):
        self.dims = [("lon", bit) for _, bit in reversed(bits_of("lon"))]
        self.dims += [("lat", bit) for _, bit in reversed(bits_of("lat"))]
        self.dims.remove(order[0])
        self.rows = keep.shape[1:]
        self.order = list(order[1:])
        self.keep = keep
        self.got = swapped(send, *order[0])

    def step(self):
        axis, bit = self.order.pop(0)
        place = self.dims.index((axis, bit))
        cut = (2,) * len(self.dims) + self.rows
        keep, got = self.keep.reshape(cut), self.got.reshape(cut)
        mine = my_bit(axis, bit)

        def total(index):
            a = lax.dynamic_index_in_dim(keep, index, place, keepdims=False)
            b = lax.dynamic_index_in_dim(got, index, place, keepdims=False)
            return (a.astype(F32) + b.astype(F32)).astype(BF)

        send = total(1 - mine)
        self.keep = total(mine)
        self.got = swapped(send, axis, bit)
        self.dims.pop(place)
        return send

    def result(self):
        while self.order:
            self.step()
        return self.keep.reshape(self.rows).astype(F32) + self.got.reshape(self.rows).astype(F32)


def cut_pieces(value, pieces, axis, mesh_axis, bit):
    stride = bit * (lax.axis_size("lat") if mesh_axis == "lon" else 1)
    size = stride * (value.shape[axis] // pieces)
    dims = (pieces // (2 * stride), 2, size)
    value = value.reshape(value.shape[:axis] + dims + value.shape[axis + 1 :])
    mine = my_bit(mesh_axis, bit)
    return [lax.dynamic_index_in_dim(value, one, axis + 1, keepdims=False) for one in (mine, 1 - mine)]


def local(fields, shift_offsets, w_embed, w_qkv, w_proj, w_head, log_scale, bias_table, cotangent):
    height, breadth, depth = fields.shape
    groups = height // WIN
    model = w_embed.shape[1]
    outputs = w_head.shape[1]
    width = w_qkv.shape[2]
    pairs = width // PAIR
    lat, mp = lax.axis_index("lat"), lax.axis_index("mp")
    rows_here = cotangent.shape[0]
    offsets = lax.dynamic_slice_in_dim(shift_offsets, lat * groups, groups)
    strip = 4
    strips = rows_here // strip
    firsts = mp * rows_here + strip * jnp.arange(strips, dtype=jnp.int32)
    strip_offsets = jnp.take(offsets, firsts // WIN)
    place = mp.reshape(1)
    pieces = lax.axis_size("lon") * lax.axis_size("lat")

    cuts = [0, 2, groups]
    tiles = fields.reshape(groups, SPAN, depth)
    tiles = [tiles[first:last] for first, last in zip(cuts[:-1], cuts[1:])]
    shifts = [offsets[first:last] for first, last in zip(cuts[:-1], cuts[1:])]
    cot = cotangent.reshape(-1, outputs)
    next_tiles = [moved(tile, "lon", -1) for tile in tiles]
    other_cot = swapped(cot, "mp", 1)

    scales = jnp.exp(jnp.minimum(log_scale, scale_cap))
    scales = jnp.repeat(scales.reshape(pairs, 1, 2), HD, axis=2)
    biases = jnp.einsum(
        "ije,he->hji", offset_onehot(WIN), bias_table, precision=lax.Precision.HIGHEST
    )
    biases = biases.reshape(pairs, 2, SPAN, SPAN).transpose(0, 2, 1, 3).reshape(pairs, SPAN, PAIR)

    half_up = half_up_call(place, cot, other_cot, w_head.T)
    next_tiles[0], half_up, biases, strip_offsets = lax.optimization_barrier(
        (next_tiles[0], half_up, biases, strip_offsets)
    )
    terms, other_terms = [], []
    for index, (shift, tile, next_tile) in enumerate(zip(shifts, tiles, next_tiles)):
        if terms:
            next_tile = after(next_tile, terms[-1])
            half_up = after(half_up, next_tile)
        terms.append(embed_call(shift, tile, next_tile, w_embed).astype(F16))
        other_terms.append(swapped(terms[-1], "mp", 1))
    half_up = half_up.reshape(groups, SPAN, -1)
    own_up = roll_call(offsets, half_up, moved(half_up, "lon", -1), 1)
    own_up = own_up.reshape(groups * SPAN, -1)
    other_up = swapped(after(own_up, other_terms[-1]), "mp", 1)

    w_parts = w_qkv.transpose(1, 0, 2)
    rolled, qkv, probs, attended = zip(
        *[forward_call(a, b, w_parts, scales, biases) for a, b in zip(terms, other_terms)]
    )
    mixed_here, mixed_there = mix_call(place, w_proj, attended)
    left_keep, left_send = [
        side.reshape(groups * SPAN, -1)
        for side in cut_pieces(jnp.concatenate(rolled, 0), pieces, 1, "lat", 1)
    ]
    all_attended = jnp.concatenate(attended, 0)
    other_up, mixed_here, left_keep, left_send, all_attended = lax.optimization_barrier(
        (other_up, mixed_here, left_keep, left_send, all_attended)
    )
    mixed_got = swapped(after(mixed_there, other_up), "mp", 1)
    up = jnp.where(
        mp == 0, jnp.concatenate([own_up, other_up], 1), jnp.concatenate([other_up, own_up], 1)
    )
    all_bits = bits_of("lat") + bits_of("lon")
    z_first = bits_of("lon")[:1] + bits_of("lat") + bits_of("lon")[1:]
    grad_p = dot(up, all_attended, 0, 0).astype(BF)
    keep, send = [
        side.reshape(pieces // 2, -1, width) for side in cut_pieces(grad_p, pieces, 0, *z_first[0])
    ]
    v_order = bits_of("lat")[:1] + bits_of("lon")[:1] + bits_of("lat")[1:] + bits_of("lon")[1:]
    sum_p = Sum(keep, send, z_first)

    d_qk, d_value = backward_call(
        place, own_up, after(other_up, send), w_proj, scales, qkv, probs
    )

    def products(left, right):
        return dot(left, right, 0, 0).astype(BF).reshape(pieces // 2, model // pieces, -1)

    pred_here, pred_there = head_call(place, after(mixed_here, d_qk), mixed_got, w_head.T, rolled)
    qk_send = products(left_send, after(d_qk, pred_there))
    sum_p.got = after(sum_p.got, qk_send)
    sent = sum_p.step()
    qk_send = after(qk_send, sent)
    v_send = products(left_send, after(d_value, qk_send))
    qk_keep = products(left_keep, after(d_qk, v_send))
    sum_qk = Sum(qk_keep, qk_send, all_bits)
    sum_qk.got = after(sum_qk.got, qk_keep)
    sent = sum_qk.step()
    sum_p.got = after(sum_p.got, sent)
    sent = sum_p.step()
    v_keep = products(left_keep, after(d_value, sent))
    sum_v = Sum(v_keep, v_send, v_order)
    sum_v.got = after(sum_v.got, v_keep)
    sent = sum_v.step()
    pred_got = after(swapped(pred_there, "mp", 1), sent)
    pred = (pred_here.astype(F32) + pred_got.astype(F32)).astype(BF)
    pred = pred.reshape(strips, strip * WIN, outputs)
    before = moved(pred, "lon", 1)
    sum_p.got = after(sum_p.got, pred)
    sent = sum_p.step()
    sum_qk.got = after(sum_qk.got, sent)
    sent = sum_qk.step()
    sum_v.got = after(sum_v.got, sent)
    sent = sum_v.step()
    before = after(before, sent)
    prediction = roll_call(strip_offsets, pred, before, -1).reshape(rows_here, breadth, outputs)
    sum_p.got = after(sum_p.got, prediction)
    grad_proj = sum_p.result().T
    sum_v.got = after(sum_v.got, grad_proj)
    sent = sum_v.step()
    sum_qk.got = after(sum_qk.got, sent)
    sent = sum_qk.step()
    sum_v.got = after(sum_v.got, sent)
    grad_v = sum_v.result()
    sum_qk.got = after(sum_qk.got, grad_v)
    grad_qk = sum_qk.result()
    grad_qkv = jnp.concatenate([grad_qk, grad_v], 1).reshape(-1, 3, width)
    return (prediction, grad_qkv, grad_proj)


def solution(mesh):
    in_specs = (
        P("lat", "lon", "mp"),
        P(),
        P("mp", None),
        P(None, None, "mp"),
        P("mp", None),
        P("mp", None),
        P("mp"),
        P("mp", None),
        P(("lat", "mp"), "lon", None),
    )
    out_specs = (
        P(("lat", "mp"), "lon", None),
        P(("lon", "lat"), None, "mp"),
        P("mp", ("lon", "lat")),
    )
    return jax.shard_map(local, mesh=mesh, in_specs=in_specs, out_specs=out_specs, check_vma=False)
```

```python
import functools

import jax
import jax.numpy as jnp
from jax import lax
from jax.experimental import pallas as pl
from jax.experimental.pallas import tpu as pltpu
from jax.sharding import PartitionSpec as P

HD = 64
WIN = 8
SPAN = WIN * WIN
PAIR = 2 * HD

eps = 1e-06
scale_cap = 4.605170185988092

BF = jnp.bfloat16
F32 = jnp.float32
F16 = jnp.float16
TERM_SCALE = 64.0
VMEM_LIMIT = 30 * 1024 * 1024
SMALL_LIMIT = 24 * 1024 * 1024


def moved(value, axis, steps):
    count = lax.axis_size(axis)
    pairs = [(source, (source + steps) % count) for source in range(count)]
    return lax.ppermute(value, axis, pairs)


def swapped(value, axis, bit):
    count = lax.axis_size(axis)
    return lax.ppermute(value, axis, [(source, source ^ bit) for source in range(count)])


def spec(space=pltpu.VMEM):
    return pl.BlockSpec(memory_space=space)


def call(body, out_shape, kinds, micros, scratch=(), limit=VMEM_LIMIT):
    return pl.pallas_call(
        body,
        out_shape=out_shape,
        in_specs=[spec(pltpu.SMEM) if kind == "s" else spec() for kind in kinds],
        out_specs=jax.tree.map(lambda _: spec(), out_shape),
        scratch_shapes=list(scratch),
        compiler_params=pltpu.CompilerParams(vmem_limit_bytes=limit),
        cost_estimate=pl.CostEstimate(flops=int(micros * 1.0e9), bytes_accessed=1, transcendentals=0),
    )


def after(value, *others):
    return lax.optimization_barrier((value,) + others)[0]


def shape(dims, dtype=BF):
    return jax.ShapeDtypeStruct(tuple(dims), dtype)


def dot(a, b, ca=1, cb=0):
    return lax.dot_general(a, b, (((ca,), (cb,)), ((), ())), preferred_element_type=F32)


def rolled_block(own, other, shift):
    size = own.shape[0]
    row = lax.broadcasted_iota(jnp.int32, (size, size), 0)
    col = lax.broadcasted_iota(jnp.int32, (size, size), 1)
    target = (row & (WIN - 1)) + shift
    same = ((row >> 3) == (col >> 3)) & ((col & (WIN - 1)) == (target & (WIN - 1)))
    inside = (target >= 0) & (target < WIN)
    mine = jnp.where(same & inside, 1.0, 0.0).astype(BF)
    theirs = jnp.where(same & ~inside, 1.0, 0.0).astype(BF)
    return (dot(mine, own) + dot(theirs, other)).astype(BF)


def roll_kernel(sign, shifts, own, other, out):
    for block in range(own.shape[0]):
        out[block] = rolled_block(own[block], other[block], sign * shifts[block])


def roll_call(shifts, own, other, sign):
    body = functools.partial(roll_kernel, sign)
    return call(body, jax.ShapeDtypeStruct(own.shape, BF), "svv", 2)(shifts, own, other)


def embed_kernel(shifts, own, other, weight, out, gathered):
    for block in range(own.shape[0]):
        gathered[pl.ds(block * SPAN, SPAN), :] = rolled_block(
            own[block], other[block], shifts[block]
        )
    out[...] = dot(gathered[...], weight[...]) * TERM_SCALE


def embed_call(shifts, own, other, weight):
    rows = own.shape[0] * SPAN
    width = weight.shape[1]
    return call(
        embed_kernel,
        jax.ShapeDtypeStruct((rows, width), F32),
        "svvv",
        5,
        [pltpu.VMEM((rows, weight.shape[0]), BF)],
    )(shifts, own, other, weight)


def halves(value):
    left = lax.broadcasted_iota(jnp.int32, value.shape, 1) < HD
    zero = jnp.zeros_like(value)
    return jnp.concatenate([jnp.where(left, value, zero), jnp.where(left, zero, value)], 0)


def joined(value):
    top = value[:SPAN]
    left = lax.broadcasted_iota(jnp.int32, top.shape, 1) < HD
    return jnp.where(left, top, value[SPAN:])


def two_parts(value):
    high = value.astype(BF)
    return high, (value - high.astype(F32)).astype(BF)


def head_ones():
    row = lax.broadcasted_iota(jnp.int32, (PAIR, PAIR), 0)
    col = lax.broadcasted_iota(jnp.int32, (PAIR, PAIR), 1)
    return jnp.where((row < HD) == (col < HD), 1.0, 0.0).astype(BF)


def short_sums(value, ones):
    return dot(value.astype(BF), ones)


def head_sums(value, ones):
    high, low = two_parts(value)
    return dot(high, ones) + dot(low, ones)


def square(value):
    wide = value.astype(F32)
    return wide * wide


def row_norms(query_halves):
    high, low = two_parts(square(query_halves))
    ones = jnp.ones((WIN, PAIR), BF)
    total = dot(ones, high, 1, 1) + dot(ones, low, 1, 1)
    return lax.rsqrt(total[:1] + eps)


def short_row_norms(query_halves):
    ones = jnp.ones((WIN, PAIR), BF)
    total = dot(ones, square(query_halves).astype(BF), 1, 1)
    return lax.rsqrt(total[:1] + eps)


def forward_kernel(rolled, w_qkv, scales, biases, qkv, probs, attended):
    width = w_qkv.shape[2]
    for part in range(3):
        qkv[:, part * width : (part + 1) * width] = dot(rolled[...], w_qkv[part]).astype(BF)
    ones = head_ones()
    pairs = width // PAIR
    for window in range(rolled.shape[0] // SPAN):
        rows = pl.ds(window * SPAN, SPAN)
        for pair in range(pairs):
            lanes = pl.ds(pair * PAIR, PAIR)
            query = qkv[rows, lanes]
            key = qkv[rows, pl.ds(width + pair * PAIR, PAIR)]
            value = qkv[rows, pl.ds(2 * width + pair * PAIR, PAIR)]
            query_halves = halves(query)
            key_norm = lax.rsqrt(head_sums(square(key), ones) + eps)
            query_norm = row_norms(query_halves) * scales[pair]
            scores = dot(key, query_halves, 1, 1) * key_norm * query_norm + biases[pair]
            weights = jnp.exp(scores - jnp.max(scores, 0, keepdims=True))
            share = weights * (1.0 / jnp.sum(weights, 0, keepdims=True))
            probs[window, pair] = share
            attended[rows, lanes] = joined(dot(share.astype(BF), value, 0, 0)).astype(BF)


def forward_call(mine, theirs, w_qkv, scales, biases):
    rolled = ((mine.astype(F32) + theirs.astype(F32)) * (1.0 / TERM_SCALE)).astype(BF)
    rows = rolled.shape[0]
    width = w_qkv.shape[2]
    pairs = width // PAIR
    out_shape = (
        shape((rows, 3 * width)),
        shape((rows // SPAN, pairs, SPAN, PAIR), F32),
        shape((rows, width)),
    )
    got = call(forward_kernel, out_shape, "vvvv", 0.05)(rolled, w_qkv, scales, biases)
    return (rolled,) + tuple(got)


def unit_grad(value, norm, grad, ones):
    wide = value.astype(F32)
    along = short_sums(wide * grad, ones)
    return norm * (grad - wide * (norm * norm) * along)


def backward_kernel(chunks, place, own_up, other_up, w_proj, scales, *refs):
    width, model = w_proj.shape
    d_qk, d_value, d_att = refs[2 * chunks :]
    half = model // 2
    mine = pl.ds(pl.multiple_of(place[0] * half, PAIR), half)
    theirs = pl.ds(pl.multiple_of((1 - place[0]) * half, PAIR), half)
    d_att[...] = (
        dot(own_up[...], w_proj[:, mine], 1, 1) + dot(other_up[...], w_proj[:, theirs], 1, 1)
    ).astype(BF)
    first = 0
    for qkv, probs in zip(refs[:chunks], refs[chunks : 2 * chunks]):
        backward_chunk(first, qkv, probs, scales, d_att, d_qk, d_value)
        first += probs.shape[0]


def backward_chunk(first, qkv, probs, scales, d_att, d_qk, d_value):
    width = d_att.shape[1]
    ones = head_ones()
    for window in range(probs.shape[0]):
        rows = pl.ds((first + window) * SPAN, SPAN)
        for pair in range(width // PAIR):
            spots = [pl.ds(part * width + pair * PAIR, PAIR) for part in range(3)]
            query, key, value = [qkv[pl.ds(window * SPAN, SPAN), spot] for spot in spots]
            query_halves = halves(query)
            key_norm = lax.rsqrt(short_sums(square(key), ones) + eps)
            query_norm = lax.rsqrt(short_sums(square(query), ones) + eps)
            query_lanes = short_row_norms(query_halves)
            share = probs[window, pair]
            grad_halves = halves(d_att[rows, pl.ds(pair * PAIR, PAIR)])
            d_value[rows, spots[0]] = dot(share.astype(BF), grad_halves).astype(BF)
            d_probs = dot(value, grad_halves, 1, 1).astype(BF).astype(F32)
            mean = jnp.sum(d_probs * share, 0, keepdims=True)
            d_cos = share * (d_probs - mean) * scales[pair]
            d_query = joined(dot((d_cos * key_norm).astype(BF), key, 0, 0))
            d_key = dot((d_cos * query_lanes).astype(BF), query_halves)
            d_qk[rows, spots[0]] = unit_grad(query, query_norm, d_query, ones).astype(BF)
            d_qk[rows, spots[1]] = unit_grad(key, key_norm, d_key, ones).astype(BF)


def backward_call(place, own_up, other_up, w_proj, scales, qkv, probs):
    rows = own_up.shape[0]
    width = w_proj.shape[0]
    return call(
        functools.partial(backward_kernel, len(qkv)),
        (shape((rows, 2 * width)), shape((rows, width))),
        "svvvv" + "vv" * len(qkv),
        9,
        [pltpu.VMEM((rows, width), BF)],
        SMALL_LIMIT,
    )(place, own_up, other_up, w_proj, scales, *qkv, *probs)


def half_up_kernel(place, own, other, w_head_t, out):
    rows = own.shape[0]
    out[pl.ds(pl.multiple_of(place[0] * rows, 32), rows), :] = dot(own[...], w_head_t[...]).astype(BF)
    out[pl.ds(pl.multiple_of((1 - place[0]) * rows, 32), rows), :] = dot(
        other[...], w_head_t[...]
    ).astype(BF)


def half_up_call(place, own, other, w_head_t):
    rows, depth = own.shape
    width = w_head_t.shape[1]
    return call(
        half_up_kernel, shape((2 * rows, width)), "svvv", 3
    )(place, own, other, w_head_t)


def mix_kernel(chunks, place, w_proj, *refs):
    att, keep, send = refs[:chunks], refs[chunks], refs[chunks + 1]
    half = w_proj.shape[1] // 2
    mine = pl.ds(pl.multiple_of(place[0] * half, PAIR), half)
    theirs = pl.ds(pl.multiple_of((1 - place[0]) * half, PAIR), half)
    start = 0
    for a in att:
        rows = pl.ds(start, a.shape[0])
        send[rows, :] = dot(a[...], w_proj[:, theirs]).astype(BF)
        keep[rows, :] = dot(a[...], w_proj[:, mine]).astype(BF)
        start += a.shape[0]


def mix_call(place, w_proj, attended):
    count = sum(a.shape[0] for a in attended)
    width, model = w_proj.shape
    out = shape((count, model // 2))
    return call(
        functools.partial(mix_kernel, len(attended)),
        (out, out),
        "sv" + "v" * len(attended),
        0.05,
    )(place, w_proj, *attended)


def head_kernel(chunks, place, mine, theirs, w_head_t, *refs):
    rolled, keep, send, merged = refs[:chunks], refs[chunks], refs[chunks + 1], refs[chunks + 2]
    half = w_head_t.shape[1]
    lanes = pl.ds(pl.multiple_of(place[0] * half, PAIR), half)
    start = 0
    for a in rolled:
        rows = pl.ds(start, a.shape[0])
        mixed = (mine[rows, :].astype(F32) + theirs[rows, :].astype(F32)).astype(BF)
        merged[rows, :] = (a[:, lanes].astype(F32) + mixed.astype(F32)).astype(BF)
        start += a.shape[0]
    count = keep.shape[0]
    own = pl.ds(pl.multiple_of(place[0] * count, 32), count)
    other = pl.ds(pl.multiple_of((1 - place[0]) * count, 32), count)
    send[...] = dot(merged[other, :], w_head_t[...], 1, 1).astype(BF)
    keep[...] = dot(merged[own, :], w_head_t[...], 1, 1).astype(BF)


def head_call(place, mine, theirs, w_head_t, rolled):
    count, half = mine.shape
    outputs = w_head_t.shape[0]
    out = shape((count // 2, outputs))
    return call(
        functools.partial(head_kernel, len(rolled)),
        (out, out),
        "svvv" + "v" * len(rolled),
        4,
        [pltpu.VMEM((count, half), BF)],
    )(place, mine, theirs, w_head_t, *rolled)


def offset_onehot(window):
    span = window * window
    places = jnp.arange(span, dtype=jnp.int32)
    across = places // window
    along = places % window
    code = (across[:, None] - across[None, :] + window - 1) * (2 * window - 1) + (
        along[:, None] - along[None, :] + window - 1
    )
    entries = jnp.arange((2 * window - 1) ** 2, dtype=jnp.int32)
    return (code[:, :, None] == entries[None, None, :]).astype(F32)


def bits_of(axis):
    bits = []
    bit = 1
    while bit < lax.axis_size(axis):
        bits.append((axis, bit))
        bit *= 2
    return bits


def my_bit(axis, bit):
    return (lax.axis_index(axis) // bit) % 2


class Sum:
    def __init__(self, keep, send, order):
        self.dims = [("lon", bit) for _, bit in reversed(bits_of("lon"))]
        self.dims += [("lat", bit) for _, bit in reversed(bits_of("lat"))]
        self.dims.remove(order[0])
        self.rows = keep.shape[1:]
        self.order = list(order[1:])
        self.keep = keep
        self.got = swapped(send, *order[0])

    def step(self):
        axis, bit = self.order.pop(0)
        place = self.dims.index((axis, bit))
        cut = (2,) * len(self.dims) + self.rows
        keep, got = self.keep.reshape(cut), self.got.reshape(cut)
        mine = my_bit(axis, bit)

        def total(index):
            a = lax.dynamic_index_in_dim(keep, index, place, keepdims=False)
            b = lax.dynamic_index_in_dim(got, index, place, keepdims=False)
            return (a.astype(F32) + b.astype(F32)).astype(BF)

        send = total(1 - mine)
        self.keep = total(mine)
        self.got = swapped(send, axis, bit)
        self.dims.pop(place)
        return send

    def result(self):
        while self.order:
            self.step()
        return self.keep.reshape(self.rows).astype(F32) + self.got.reshape(self.rows).astype(F32)


def cut_pieces(value, pieces, axis, mesh_axis, bit):
    stride = bit * (lax.axis_size("lat") if mesh_axis == "lon" else 1)
    size = stride * (value.shape[axis] // pieces)
    dims = (pieces // (2 * stride), 2, size)
    value = value.reshape(value.shape[:axis] + dims + value.shape[axis + 1 :])
    mine = my_bit(mesh_axis, bit)
    return [lax.dynamic_index_in_dim(value, one, axis + 1, keepdims=False) for one in (mine, 1 - mine)]


def local(fields, shift_offsets, w_embed, w_qkv, w_proj, w_head, log_scale, bias_table, cotangent):
    height, breadth, depth = fields.shape
    groups = height // WIN
    model = w_embed.shape[1]
    outputs = w_head.shape[1]
    width = w_qkv.shape[2]
    pairs = width // PAIR
    lat, mp = lax.axis_index("lat"), lax.axis_index("mp")
    rows_here = cotangent.shape[0]
    offsets = lax.dynamic_slice_in_dim(shift_offsets, lat * groups, groups)
    strip = 4
    strips = rows_here // strip
    firsts = mp * rows_here + strip * jnp.arange(strips, dtype=jnp.int32)
    strip_offsets = jnp.take(offsets, firsts // WIN)
    place = mp.reshape(1)
    pieces = lax.axis_size("lon") * lax.axis_size("lat")

    cuts = [0, 2, groups]
    tiles = fields.reshape(groups, SPAN, depth)
    tiles = [tiles[first:last] for first, last in zip(cuts[:-1], cuts[1:])]
    shifts = [offsets[first:last] for first, last in zip(cuts[:-1], cuts[1:])]
    cot = cotangent.reshape(-1, outputs)
    next_tiles = [moved(tile, "lon", -1) for tile in tiles]
    other_cot = swapped(cot, "mp", 1)

    scales = jnp.exp(jnp.minimum(log_scale, scale_cap))
    scales = jnp.repeat(scales.reshape(pairs, 1, 2), HD, axis=2)
    biases = jnp.einsum(
        "ije,he->hji", offset_onehot(WIN), bias_table, precision=lax.Precision.HIGHEST
    )
    biases = biases.reshape(pairs, 2, SPAN, SPAN).transpose(0, 2, 1, 3).reshape(pairs, SPAN, PAIR)

    next_tiles[0], biases, strip_offsets = lax.optimization_barrier(
        (next_tiles[0], biases, strip_offsets)
    )
    terms, other_terms = [], []
    for index, (shift, tile, next_tile) in enumerate(zip(shifts, tiles, next_tiles)):
        terms.append(embed_call(shift, tile, next_tile, w_embed).astype(F16))
        other_terms.append(swapped(terms[-1], "mp", 1))
    half_up = half_up_call(place, cot, after(other_cot, terms[0]), w_head.T)
    half_up = after(half_up, terms[1]).reshape(groups, SPAN, -1)
    own_up = roll_call(offsets, half_up, moved(half_up, "lon", -1), 1)
    own_up = own_up.reshape(groups * SPAN, -1)
    other_up = swapped(after(own_up, other_terms[-1]), "mp", 1)

    w_parts = w_qkv.transpose(1, 0, 2)
    rolled, qkv, probs, attended = zip(
        *[forward_call(a, b, w_parts, scales, biases) for a, b in zip(terms, other_terms)]
    )
    mixed_here, mixed_there = mix_call(place, w_proj, attended)
    left_keep, left_send = [
        side.reshape(groups * SPAN, -1)
        for side in cut_pieces(jnp.concatenate(rolled, 0), pieces, 1, "lat", 1)
    ]
    all_attended = jnp.concatenate(attended, 0)
    other_up, mixed_here, left_keep, left_send, all_attended = lax.optimization_barrier(
        (other_up, mixed_here, left_keep, left_send, all_attended)
    )
    mixed_got = swapped(after(mixed_there, other_up), "mp", 1)
    up = jnp.where(
        mp == 0, jnp.concatenate([own_up, other_up], 1), jnp.concatenate([other_up, own_up], 1)
    )
    all_bits = bits_of("lat") + bits_of("lon")
    z_first = bits_of("lon")[:1] + bits_of("lat") + bits_of("lon")[1:]
    grad_p = dot(up, all_attended, 0, 0).astype(BF)
    keep, send = [
        side.reshape(pieces // 2, -1, width) for side in cut_pieces(grad_p, pieces, 0, *z_first[0])
    ]
    v_order = bits_of("lat")[:1] + bits_of("lon")[:1] + bits_of("lat")[1:] + bits_of("lon")[1:]
    sum_p = Sum(keep, send, z_first)

    d_qk, d_value = backward_call(
        place, own_up, after(other_up, send), w_proj, scales, qkv, probs
    )

    def products(left, right):
        return dot(left, right, 0, 0).astype(BF).reshape(pieces // 2, model // pieces, -1)

    v_send = products(left_send, d_value)
    pred_here, pred_there = head_call(
        place, after(mixed_here, v_send, d_qk), mixed_got, w_head.T, rolled
    )
    qk_send = products(left_send, after(d_qk, pred_there))
    sum_p.got = after(sum_p.got, qk_send)
    sent = sum_p.step()
    qk_send = after(qk_send, sent)
    v_keep = products(left_keep, after(d_value, qk_send))
    sum_v = Sum(v_keep, v_send, v_order)
    sent = sum_v.step()
    qk_keep = products(left_keep, after(d_qk, sent))
    sum_qk = Sum(qk_keep, qk_send, all_bits)
    sum_qk.got = after(sum_qk.got, qk_keep)
    sent = sum_qk.step()
    pred_got = after(swapped(pred_there, "mp", 1), sent)
    pred = (pred_here.astype(F32) + pred_got.astype(F32)).astype(BF)
    pred = pred.reshape(strips, strip * WIN, outputs)
    before = moved(pred, "lon", 1)
    sum_p.got = after(sum_p.got, pred)
    sent = sum_p.step()
    sum_qk.got = after(sum_qk.got, sent)
    sent = sum_qk.step()
    sum_v.got = after(sum_v.got, sent)
    sent = sum_v.step()
    sum_p.got = after(sum_p.got, sent)
    sent = sum_p.step()
    before = after(before, sent)
    prediction = roll_call(strip_offsets, pred, before, -1).reshape(rows_here, breadth, outputs)
    sum_v.got = after(sum_v.got, prediction)
    sent = sum_v.step()
    sum_qk.got = after(sum_qk.got, sent)
    sent = sum_qk.step()
    sum_p.got = after(sum_p.got, sent)
    grad_proj = sum_p.result().T
    sum_v.got = after(sum_v.got, grad_proj)
    grad_v = sum_v.result()
    sum_qk.got = after(sum_qk.got, grad_v)
    grad_qk = sum_qk.result()
    grad_qkv = jnp.concatenate([grad_qk, grad_v], 1).reshape(-1, 3, width)
    return (prediction, grad_qkv, grad_proj)


def solution(mesh):
    in_specs = (
        P("lat", "lon", "mp"),
        P(),
        P("mp", None),
        P(None, None, "mp"),
        P("mp", None),
        P("mp", None),
        P("mp"),
        P("mp", None),
        P(("lat", "mp"), "lon", None),
    )
    out_specs = (
        P(("lat", "mp"), "lon", None),
        P(("lon", "lat"), None, "mp"),
        P("mp", ("lon", "lat")),
    )
    return jax.shard_map(local, mesh=mesh, in_specs=in_specs, out_specs=out_specs, check_vma=False)
```

```python
import functools

import jax
import jax.numpy as jnp
from jax import lax
from jax.experimental import pallas as pl
from jax.experimental.pallas import tpu as pltpu
from jax.sharding import PartitionSpec as P

HD = 64
WIN = 8
SPAN = WIN * WIN
PAIR = 2 * HD

eps = 1e-06
scale_cap = 4.605170185988092

BF = jnp.bfloat16
F32 = jnp.float32
F16 = jnp.float16
TERM_SCALE = 64.0
VMEM_LIMIT = 38 * 1024 * 1024
SMALL_LIMIT = 24 * 1024 * 1024


def moved(value, axis, steps):
    count = lax.axis_size(axis)
    pairs = [(source, (source + steps) % count) for source in range(count)]
    return lax.ppermute(value, axis, pairs)


def swapped(value, axis, bit):
    count = lax.axis_size(axis)
    return lax.ppermute(value, axis, [(source, source ^ bit) for source in range(count)])


def spec(space=pltpu.VMEM):
    return pl.BlockSpec(memory_space=space)


def call(body, out_shape, kinds, micros, scratch=(), limit=VMEM_LIMIT):
    return pl.pallas_call(
        body,
        out_shape=out_shape,
        in_specs=[spec(pltpu.SMEM) if kind == "s" else spec() for kind in kinds],
        out_specs=jax.tree.map(lambda _: spec(), out_shape),
        scratch_shapes=list(scratch),
        compiler_params=pltpu.CompilerParams(vmem_limit_bytes=limit),
        cost_estimate=pl.CostEstimate(flops=int(micros * 1.0e9), bytes_accessed=1, transcendentals=0),
    )


def after(value, *others):
    return lax.optimization_barrier((value,) + others)[0]


def shape(dims, dtype=BF):
    return jax.ShapeDtypeStruct(tuple(dims), dtype)


def dot(a, b, ca=1, cb=0):
    return lax.dot_general(a, b, (((ca,), (cb,)), ((), ())), preferred_element_type=F32)


def rolled_block(own, other, shift):
    size = own.shape[0]
    row = lax.broadcasted_iota(jnp.int32, (size, size), 0)
    col = lax.broadcasted_iota(jnp.int32, (size, size), 1)
    target = (row & (WIN - 1)) + shift
    same = ((row >> 3) == (col >> 3)) & ((col & (WIN - 1)) == (target & (WIN - 1)))
    inside = (target >= 0) & (target < WIN)
    mine = jnp.where(same & inside, 1.0, 0.0).astype(BF)
    theirs = jnp.where(same & ~inside, 1.0, 0.0).astype(BF)
    return (dot(mine, own) + dot(theirs, other)).astype(BF)


def roll_kernel(sign, shifts, own, other, out):
    for block in range(own.shape[0]):
        out[block] = rolled_block(own[block], other[block], sign * shifts[block])


def roll_call(shifts, own, other, sign):
    body = functools.partial(roll_kernel, sign)
    return call(body, jax.ShapeDtypeStruct(own.shape, BF), "svv", 2)(shifts, own, other)


def embed_kernel(shifts, own, other, weight, out, gathered):
    for block in range(own.shape[0]):
        gathered[pl.ds(block * SPAN, SPAN), :] = rolled_block(
            own[block], other[block], shifts[block]
        )
    out[...] = dot(gathered[...], weight[...]) * TERM_SCALE


def embed_call(shifts, own, other, weight):
    rows = own.shape[0] * SPAN
    width = weight.shape[1]
    return call(
        embed_kernel,
        jax.ShapeDtypeStruct((rows, width), F32),
        "svvv",
        5,
        [pltpu.VMEM((rows, weight.shape[0]), BF)],
    )(shifts, own, other, weight)


def halves(value):
    left = lax.broadcasted_iota(jnp.int32, value.shape, 1) < HD
    zero = jnp.zeros_like(value)
    return jnp.concatenate([jnp.where(left, value, zero), jnp.where(left, zero, value)], 0)


def joined(value):
    top = value[:SPAN]
    left = lax.broadcasted_iota(jnp.int32, top.shape, 1) < HD
    return jnp.where(left, top, value[SPAN:])


def two_parts(value):
    high = value.astype(BF)
    return high, (value - high.astype(F32)).astype(BF)


def head_ones():
    row = lax.broadcasted_iota(jnp.int32, (PAIR, PAIR), 0)
    col = lax.broadcasted_iota(jnp.int32, (PAIR, PAIR), 1)
    return jnp.where((row < HD) == (col < HD), 1.0, 0.0).astype(BF)


def short_sums(value, ones):
    return dot(value.astype(BF), ones)


def head_sums(value, ones):
    high, low = two_parts(value)
    return dot(high, ones) + dot(low, ones)


def square(value):
    wide = value.astype(F32)
    return wide * wide


def row_norms(query_halves):
    high, low = two_parts(square(query_halves))
    ones = jnp.ones((WIN, PAIR), BF)
    total = dot(ones, high, 1, 1) + dot(ones, low, 1, 1)
    return lax.rsqrt(total[:1] + eps)


def short_row_norms(query_halves):
    ones = jnp.ones((WIN, PAIR), BF)
    total = dot(ones, square(query_halves).astype(BF), 1, 1)
    return lax.rsqrt(total[:1] + eps)


def forward_kernel(rolled, w_qkv, scales, biases, qkv, probs, attended):
    width = w_qkv.shape[2]
    for part in range(3):
        qkv[:, part * width : (part + 1) * width] = dot(rolled[...], w_qkv[part]).astype(BF)
    ones = head_ones()
    pairs = width // PAIR
    for window in range(rolled.shape[0] // SPAN):
        rows = pl.ds(window * SPAN, SPAN)
        for pair in range(pairs):
            lanes = pl.ds(pair * PAIR, PAIR)
            query = qkv[rows, lanes]
            key = qkv[rows, pl.ds(width + pair * PAIR, PAIR)]
            value = qkv[rows, pl.ds(2 * width + pair * PAIR, PAIR)]
            query_halves = halves(query)
            key_norm = lax.rsqrt(head_sums(square(key), ones) + eps)
            query_norm = row_norms(query_halves) * scales[pair]
            scores = dot(key, query_halves, 1, 1) * key_norm * query_norm + biases[pair]
            weights = jnp.exp(scores - jnp.max(scores, 0, keepdims=True))
            share = weights * (1.0 / jnp.sum(weights, 0, keepdims=True))
            probs[window, pair] = share
            attended[rows, lanes] = joined(dot(share.astype(BF), value, 0, 0)).astype(BF)


def forward_call(mine, theirs, w_qkv, scales, biases):
    rolled = ((mine.astype(F32) + theirs.astype(F32)) * (1.0 / TERM_SCALE)).astype(BF)
    rows = rolled.shape[0]
    width = w_qkv.shape[2]
    pairs = width // PAIR
    out_shape = (
        shape((rows, 3 * width)),
        shape((rows // SPAN, pairs, SPAN, PAIR), F32),
        shape((rows, width)),
    )
    got = call(forward_kernel, out_shape, "vvvv", 0.05)(rolled, w_qkv, scales, biases)
    return (rolled,) + tuple(got)


def unit_grad(value, norm, grad, ones):
    wide = value.astype(F32)
    along = short_sums(wide * grad, ones)
    return norm * (grad - wide * (norm * norm) * along)


def backward_kernel(chunks, place, own_up, other_up, w_proj, scales, *refs):
    width, model = w_proj.shape
    d_qk, d_value, d_att = refs[2 * chunks :]
    half = model // 2
    mine = pl.ds(pl.multiple_of(place[0] * half, PAIR), half)
    theirs = pl.ds(pl.multiple_of((1 - place[0]) * half, PAIR), half)
    d_att[...] = (
        dot(own_up[...], w_proj[:, mine], 1, 1) + dot(other_up[...], w_proj[:, theirs], 1, 1)
    ).astype(BF)
    first = 0
    for qkv, probs in zip(refs[:chunks], refs[chunks : 2 * chunks]):
        backward_chunk(first, qkv, probs, scales, d_att, d_qk, d_value)
        first += probs.shape[0]


def backward_chunk(first, qkv, probs, scales, d_att, d_qk, d_value):
    width = d_att.shape[1]
    ones = head_ones()
    for window in range(probs.shape[0]):
        rows = pl.ds((first + window) * SPAN, SPAN)
        for pair in range(width // PAIR):
            spots = [pl.ds(part * width + pair * PAIR, PAIR) for part in range(3)]
            query, key, value = [qkv[pl.ds(window * SPAN, SPAN), spot] for spot in spots]
            query_halves = halves(query)
            key_norm = lax.rsqrt(short_sums(square(key), ones) + eps)
            query_norm = lax.rsqrt(short_sums(square(query), ones) + eps)
            query_lanes = short_row_norms(query_halves)
            share = probs[window, pair]
            grad_halves = halves(d_att[rows, pl.ds(pair * PAIR, PAIR)])
            d_value[rows, spots[0]] = dot(share.astype(BF), grad_halves).astype(BF)
            d_probs = dot(value, grad_halves, 1, 1).astype(BF).astype(F32)
            mean = jnp.sum(d_probs * share, 0, keepdims=True)
            d_cos = share * (d_probs - mean) * scales[pair]
            d_query = joined(dot((d_cos * key_norm).astype(BF), key, 0, 0))
            d_key = dot((d_cos * query_lanes).astype(BF), query_halves)
            d_qk[rows, spots[0]] = unit_grad(query, query_norm, d_query, ones).astype(BF)
            d_qk[rows, spots[1]] = unit_grad(key, key_norm, d_key, ones).astype(BF)


def backward_call(place, own_up, other_up, w_proj, scales, qkv, probs):
    rows = own_up.shape[0]
    width = w_proj.shape[0]
    return call(
        functools.partial(backward_kernel, len(qkv)),
        (shape((rows, 2 * width)), shape((rows, width))),
        "svvvv" + "vv" * len(qkv),
        9,
        [pltpu.VMEM((rows, width), BF)],
        SMALL_LIMIT,
    )(place, own_up, other_up, w_proj, scales, *qkv, *probs)


def half_up_kernel(place, own, other, w_head_t, out):
    rows = own.shape[0]
    out[pl.ds(pl.multiple_of(place[0] * rows, 32), rows), :] = dot(own[...], w_head_t[...]).astype(BF)
    out[pl.ds(pl.multiple_of((1 - place[0]) * rows, 32), rows), :] = dot(
        other[...], w_head_t[...]
    ).astype(BF)


def half_up_call(place, own, other, w_head_t):
    rows, depth = own.shape
    width = w_head_t.shape[1]
    return call(
        half_up_kernel, shape((2 * rows, width)), "svvv", 3
    )(place, own, other, w_head_t)


def mix_kernel(chunks, place, w_proj, *refs):
    att, keep, send = refs[:chunks], refs[chunks], refs[chunks + 1]
    half = w_proj.shape[1] // 2
    mine = pl.ds(pl.multiple_of(place[0] * half, PAIR), half)
    theirs = pl.ds(pl.multiple_of((1 - place[0]) * half, PAIR), half)
    start = 0
    for a in att:
        rows = pl.ds(start, a.shape[0])
        send[rows, :] = dot(a[...], w_proj[:, theirs]).astype(BF)
        keep[rows, :] = dot(a[...], w_proj[:, mine]).astype(BF)
        start += a.shape[0]


def mix_call(place, w_proj, attended):
    count = sum(a.shape[0] for a in attended)
    width, model = w_proj.shape
    out = shape((count, model // 2))
    return call(
        functools.partial(mix_kernel, len(attended)),
        (out, out),
        "sv" + "v" * len(attended),
        0.05,
    )(place, w_proj, *attended)


def head_kernel(chunks, place, mine, theirs, w_head_t, *refs):
    rolled, keep, send, merged = refs[:chunks], refs[chunks], refs[chunks + 1], refs[chunks + 2]
    half = w_head_t.shape[1]
    lanes = pl.ds(pl.multiple_of(place[0] * half, PAIR), half)
    start = 0
    for a in rolled:
        rows = pl.ds(start, a.shape[0])
        mixed = (mine[rows, :].astype(F32) + theirs[rows, :].astype(F32)).astype(BF)
        merged[rows, :] = (a[:, lanes].astype(F32) + mixed.astype(F32)).astype(BF)
        start += a.shape[0]
    count = keep.shape[0]
    own = pl.ds(pl.multiple_of(place[0] * count, 32), count)
    other = pl.ds(pl.multiple_of((1 - place[0]) * count, 32), count)
    send[...] = dot(merged[other, :], w_head_t[...], 1, 1).astype(BF)
    keep[...] = dot(merged[own, :], w_head_t[...], 1, 1).astype(BF)


def head_call(place, mine, theirs, w_head_t, rolled):
    count, half = mine.shape
    outputs = w_head_t.shape[0]
    out = shape((count // 2, outputs))
    return call(
        functools.partial(head_kernel, len(rolled)),
        (out, out),
        "svvv" + "v" * len(rolled),
        4,
        [pltpu.VMEM((count, half), BF)],
    )(place, mine, theirs, w_head_t, *rolled)


def offset_onehot(window):
    span = window * window
    places = jnp.arange(span, dtype=jnp.int32)
    across = places // window
    along = places % window
    code = (across[:, None] - across[None, :] + window - 1) * (2 * window - 1) + (
        along[:, None] - along[None, :] + window - 1
    )
    entries = jnp.arange((2 * window - 1) ** 2, dtype=jnp.int32)
    return (code[:, :, None] == entries[None, None, :]).astype(F32)


def bits_of(axis):
    bits = []
    bit = 1
    while bit < lax.axis_size(axis):
        bits.append((axis, bit))
        bit *= 2
    return bits


def my_bit(axis, bit):
    return (lax.axis_index(axis) // bit) % 2


class Sum:
    def __init__(self, keep, send, order):
        self.dims = [("lon", bit) for _, bit in reversed(bits_of("lon"))]
        self.dims += [("lat", bit) for _, bit in reversed(bits_of("lat"))]
        self.dims.remove(order[0])
        self.rows = keep.shape[1:]
        self.order = list(order[1:])
        self.keep = keep
        self.got = swapped(send, *order[0])

    def step(self):
        axis, bit = self.order.pop(0)
        place = self.dims.index((axis, bit))
        cut = (2,) * len(self.dims) + self.rows
        keep, got = self.keep.reshape(cut), self.got.reshape(cut)
        mine = my_bit(axis, bit)

        def total(index):
            a = lax.dynamic_index_in_dim(keep, index, place, keepdims=False)
            b = lax.dynamic_index_in_dim(got, index, place, keepdims=False)
            return (a.astype(F32) + b.astype(F32)).astype(BF)

        send = total(1 - mine)
        self.keep = total(mine)
        self.got = swapped(send, axis, bit)
        self.dims.pop(place)
        return send

    def result(self):
        while self.order:
            self.step()
        return self.keep.reshape(self.rows).astype(F32) + self.got.reshape(self.rows).astype(F32)


def cut_pieces(value, pieces, axis, mesh_axis, bit):
    stride = bit * (lax.axis_size("lat") if mesh_axis == "lon" else 1)
    size = stride * (value.shape[axis] // pieces)
    dims = (pieces // (2 * stride), 2, size)
    value = value.reshape(value.shape[:axis] + dims + value.shape[axis + 1 :])
    mine = my_bit(mesh_axis, bit)
    return [lax.dynamic_index_in_dim(value, one, axis + 1, keepdims=False) for one in (mine, 1 - mine)]


def local(fields, shift_offsets, w_embed, w_qkv, w_proj, w_head, log_scale, bias_table, cotangent):
    height, breadth, depth = fields.shape
    groups = height // WIN
    model = w_embed.shape[1]
    outputs = w_head.shape[1]
    width = w_qkv.shape[2]
    pairs = width // PAIR
    lat, mp = lax.axis_index("lat"), lax.axis_index("mp")
    rows_here = cotangent.shape[0]
    offsets = lax.dynamic_slice_in_dim(shift_offsets, lat * groups, groups)
    strip = 4
    strips = rows_here // strip
    firsts = mp * rows_here + strip * jnp.arange(strips, dtype=jnp.int32)
    strip_offsets = jnp.take(offsets, firsts // WIN)
    place = mp.reshape(1)
    pieces = lax.axis_size("lon") * lax.axis_size("lat")

    cuts = [0, 2, groups]
    tiles = fields.reshape(groups, SPAN, depth)
    tiles = [tiles[first:last] for first, last in zip(cuts[:-1], cuts[1:])]
    shifts = [offsets[first:last] for first, last in zip(cuts[:-1], cuts[1:])]
    cot = cotangent.reshape(-1, outputs)
    next_tiles = [moved(tile, "lon", -1) for tile in tiles]
    other_cot = swapped(cot, "mp", 1)

    scales = jnp.exp(jnp.minimum(log_scale, scale_cap))
    scales = jnp.repeat(scales.reshape(pairs, 1, 2), HD, axis=2)
    biases = jnp.einsum(
        "ije,he->hji", offset_onehot(WIN), bias_table, precision=lax.Precision.HIGHEST
    )
    biases = biases.reshape(pairs, 2, SPAN, SPAN).transpose(0, 2, 1, 3).reshape(pairs, SPAN, PAIR)

    next_tiles[0], biases, strip_offsets = lax.optimization_barrier(
        (next_tiles[0], biases, strip_offsets)
    )
    terms, other_terms = [], []
    for index, (shift, tile, next_tile) in enumerate(zip(shifts, tiles, next_tiles)):
        terms.append(embed_call(shift, tile, next_tile, w_embed).astype(F16))
        other_terms.append(swapped(terms[-1], "mp", 1))
    half_up = half_up_call(place, cot, after(other_cot, terms[0]), w_head.T)
    half_up = after(half_up, terms[1]).reshape(groups, SPAN, -1)
    own_up = roll_call(offsets, half_up, moved(half_up, "lon", -1), 1)
    own_up = own_up.reshape(groups * SPAN, -1)
    other_up = swapped(after(own_up, other_terms[-1]), "mp", 1)

    w_parts = w_qkv.transpose(1, 0, 2)
    rolled, qkv, probs, attended = zip(
        *[forward_call(a, b, w_parts, scales, biases) for a, b in zip(terms, other_terms)]
    )
    mixed_here, mixed_there = mix_call(place, w_proj, attended)
    left_keep, left_send = [
        side.reshape(groups * SPAN, -1)
        for side in cut_pieces(jnp.concatenate(rolled, 0), pieces, 1, "lat", 1)
    ]
    all_attended = jnp.concatenate(attended, 0)
    other_up, mixed_here, left_keep, left_send, all_attended = lax.optimization_barrier(
        (other_up, mixed_here, left_keep, left_send, all_attended)
    )
    mixed_got = swapped(after(mixed_there, other_up), "mp", 1)
    up = jnp.where(
        mp == 0, jnp.concatenate([own_up, other_up], 1), jnp.concatenate([other_up, own_up], 1)
    )
    all_bits = bits_of("lat") + bits_of("lon")
    z_first = bits_of("lon")[:1] + bits_of("lat") + bits_of("lon")[1:]
    grad_p = dot(up, all_attended, 0, 0).astype(BF)
    keep, send = [
        side.reshape(pieces // 2, -1, width) for side in cut_pieces(grad_p, pieces, 0, *z_first[0])
    ]
    v_order = bits_of("lat")[:1] + bits_of("lon")[:1] + bits_of("lat")[1:] + bits_of("lon")[1:]
    sum_p = Sum(keep, send, z_first)

    d_qk, d_value = backward_call(
        place, own_up, after(other_up, send), w_proj, scales, qkv, probs
    )

    def products(left, right):
        return dot(left, right, 0, 0).astype(BF).reshape(pieces // 2, model // pieces, -1)

    v_send = products(left_send, d_value)
    pred_here, pred_there = head_call(
        place, after(mixed_here, v_send, d_qk), mixed_got, w_head.T, rolled
    )
    qk_send = products(left_send, after(d_qk, pred_there))
    sum_p.got = after(sum_p.got, qk_send)
    sent = sum_p.step()
    qk_send = after(qk_send, sent)
    v_keep = products(left_keep, after(d_value, qk_send))
    sum_v = Sum(v_keep, v_send, v_order)
    sent = sum_v.step()
    qk_keep = products(left_keep, after(d_qk, sent))
    sum_qk = Sum(qk_keep, qk_send, all_bits)
    sum_qk.got = after(sum_qk.got, qk_keep)
    sent = sum_qk.step()
    pred_got = after(swapped(pred_there, "mp", 1), sent)
    pred = (pred_here.astype(F32) + pred_got.astype(F32)).astype(BF)
    pred = pred.reshape(strips, strip * WIN, outputs)
    before = moved(pred, "lon", 1)
    sum_p.got = after(sum_p.got, pred)
    sent = sum_p.step()
    sum_qk.got = after(sum_qk.got, sent)
    sent = sum_qk.step()
    sum_v.got = after(sum_v.got, sent)
    sent = sum_v.step()
    sum_p.got = after(sum_p.got, sent)
    sent = sum_p.step()
    before = after(before, sent)
    prediction = roll_call(strip_offsets, pred, before, -1).reshape(rows_here, breadth, outputs)
    sum_v.got = after(sum_v.got, prediction)
    sent = sum_v.step()
    sum_qk.got = after(sum_qk.got, sent)
    sent = sum_qk.step()
    sum_p.got = after(sum_p.got, sent)
    grad_proj = sum_p.result().T
    sum_v.got = after(sum_v.got, grad_proj)
    grad_v = sum_v.result()
    sum_qk.got = after(sum_qk.got, grad_v)
    grad_qk = sum_qk.result()
    grad_qkv = jnp.concatenate([grad_qk, grad_v], 1).reshape(-1, 3, width)
    return (prediction, grad_qkv, grad_proj)


def solution(mesh):
    in_specs = (
        P("lat", "lon", "mp"),
        P(),
        P("mp", None),
        P(None, None, "mp"),
        P("mp", None),
        P("mp", None),
        P("mp"),
        P("mp", None),
        P(("lat", "mp"), "lon", None),
    )
    out_specs = (
        P(("lat", "mp"), "lon", None),
        P(("lon", "lat"), None, "mp"),
        P("mp", ("lon", "lat")),
    )
    return jax.shard_map(local, mesh=mesh, in_specs=in_specs, out_specs=out_specs, check_vma=False)
```
